256 devices in a mesh: row: 8 (over y_hi, x), col: 32 (over y_lo, z, core).
Axes of the slice: x: 4, y: 4 (y_hi: 2, y_lo: 2; y = y_hi * 2 + y_lo), z: 8, core: 2. Of those that a mesh axis runs over, the one named last changes fastest.
Arguments:
- layer_input: bfloat16 [1024, 12288], P(('row', 'col')), may hold values from -6 to 6
- grad_y: bfloat16 [1024, 12288], P(('row', 'col')), may hold values from -6 to 6
- norm_gain: float32 [12288], replicated, may hold values from 0.25 to 1.75
- up_bias: float32 [49152], P('col'), may hold values from -3 to 3
- up_tiles: bfloat16 [384, 8, 128, 128], P('col', 'row'), may hold values from -0.1875 to 0.1875
- down_tiles: bfloat16 [384, 8, 128, 128], P('col', 'row'), may hold values from -1 to 1
- block_cols: int32 [384, 8], P('col'), may hold values from 0 to 95, as said below
- block_count: int32 [384], P('col'), may hold values from 1 to 8
Outputs:
- layer_output: bfloat16 [1024, 12288], P(('row', 'col'))
- grad_x: bfloat16 [1024, 12288], P(('row', 'col'))
- grad_gain: float32 [12288], replicated
- grad_bias: float32 [49152], P('col')
- grad_up: float32 [384, 8, 128, 128], P('col', 'row')
- grad_down: float32 [384, 8, 128, 128], P('col', 'row')
The draws below stay inside these ranges and needn't reach their ends.
Inputs may be any that keep to these rules, and one draw needn't show every extreme that they name: `block_cols`: row i names the width blocks of the nonzero tiles of hidden block i: entries k < block_count[i] are distinct, later entries repeat entry 0.
All inputs are finite; a program needn't handle non-finite values.
Results may differ from the reference program's by a relative error of at most 0.022.
Values may be sent and summed in bfloat16 or wider, within the bound.
No kernel may reach another device: no remote copies, remote signals or barrier semaphores. Data moves between devices by JAX's collectives and lax.ppermute only.
A program may use at most 128 MiB of HBM per device.

```python
import math
import jax
import jax.numpy as jnp
from jax import lax

D = 12288
FF = 49152
BS = 128
KMAX = 8
FFB = 384
TOKENS = 1024
N_ROW = 8
N_COL = 32


def butterfly_pattern(key):
    base_key = jax.random.fold_in(key, 4242)
    label_key, anchor_key, coin_key = jax.random.split(base_key, 3)
    blocks_wide = D // BS
    blocks_hidden = FF // BS
    labels = jax.random.permutation(label_key, blocks_wide).astype(jnp.int32)
    anchor = jax.random.randint(anchor_key, (), 0, blocks_wide - 2 ** (KMAX - 2), dtype=jnp.int32)
    bases = jnp.arange(blocks_hidden, dtype=jnp.int32) % blocks_wide
    powers = jnp.left_shift(jnp.ones((KMAX - 1,), jnp.int32), jnp.arange(KMAX - 1, dtype=jnp.int32))
    partners = jnp.bitwise_xor(bases[:, None], powers[None, :])
    candidates = jnp.concatenate([bases[:, None], partners], axis=1)
    inside = candidates < blocks_wide
    coins = jax.random.randint(coin_key, (blocks_hidden, KMAX), 0, 4, dtype=jnp.int32) > 0
    keep_flags = inside & (coins | (bases == anchor)[:, None])
    keep_flags = keep_flags.at[:, 0].set(True)
    scores = jnp.where(keep_flags, 0, KMAX).astype(jnp.int32) + jnp.arange(KMAX, dtype=jnp.int32)[None, :]
    order = jnp.argsort(scores, axis=1, stable=True)
    sorted_cand = jnp.take_along_axis(candidates, order, axis=1)
    sorted_keep = jnp.take_along_axis(keep_flags, order, axis=1)
    counts = jnp.sum(keep_flags.astype(jnp.int32), axis=1)
    filled = jnp.where(sorted_keep, sorted_cand, bases[:, None])
    return (labels[filled].astype(jnp.int32), counts.astype(jnp.int32))


def draw_block_cols(key, part):
    return butterfly_pattern(key)[0]


def draw_block_count(key, part):
    return butterfly_pattern(key)[1]


def level_of(key, dims, cuts, least, top_value):
    def one(dim, blocks):
        steps = jax.random.uniform(jax.random.fold_in(jax.random.fold_in(key, 6), dim), (blocks,), jnp.float32, least / len(cuts), top_value / len(cuts))
        return jnp.repeat(jnp.exp(steps), dims[dim] // blocks).reshape((-1,) + (1,) * (len(dims) - dim - 1))

    factor_of = one(*cuts[0])
    for cut in cuts[1:]:
        factor_of = factor_of * one(*cut)
    return factor_of


def noise(key, shape, width, limit, cuts=(), held_as=jnp.bfloat16):
    level = level_of(key, shape, cuts, -0.22, 0.18) if cuts else 1.0
    array = jax.random.normal(key, shape, jnp.float32) * width * level
    return jnp.minimum(jnp.maximum(array, -limit), limit).astype(held_as)


def setup_inputs(seed: int = 0) -> dict:
    arg_keys = jax.random.split(jax.random.key(seed), 9)
    layer_input = noise(arg_keys[0], (TOKENS, D), 1.0, 6.0, ((0, 256),))
    grad_y = noise(arg_keys[1], (TOKENS, D), 1.0, 6.0, ((0, 256),))
    norm_gain = jnp.clip(1.0 + 0.15 * jax.random.normal(arg_keys[2], (D,), jnp.float32), 0.25, 1.75)
    up_bias = noise(arg_keys[3], (FF,), 0.5, 3.0, ((0, 32),), jnp.float32)
    up_tiles = noise(arg_keys[4], (FFB, KMAX, BS, BS), (KMAX * BS) ** -0.5, 0.1875, ((0, 32), (1, 8)))
    down_tiles = noise(arg_keys[5], (FFB, KMAX, BS, BS), (FF * KMAX // D * BS // BS) ** -0.5, 1.0, ((0, 32), (1, 8)))
    block_cols = draw_block_cols(jax.random.fold_in(arg_keys[8], 71), 0)
    block_count = draw_block_count(jax.random.fold_in(arg_keys[8], 71), 0)
    return dict(layer_input=layer_input, grad_y=grad_y, norm_gain=norm_gain, up_bias=up_bias, up_tiles=up_tiles, down_tiles=down_tiles, block_cols=block_cols, block_count=block_count)


NORM_EPS = 1e-05
GELU_COEF = math.sqrt(2.0 / math.pi)
CUBIC_COEF = 0.044715

def gelu_tanh(values):
    return 0.5 * values * (1.0 + jnp.tanh(GELU_COEF * (values + CUBIC_COEF * values * values * values)))

def gelu_slope(values):
    bent = jnp.tanh(GELU_COEF * (values + CUBIC_COEF * values * values * values))
    return 0.5 * (1.0 + bent) + 0.5 * values * (1.0 - bent * bent) * GELU_COEF * (1.0 + 3.0 * CUBIC_COEF * values * values)

def rounded(values):
    return lax.optimization_barrier(values.astype(jnp.bfloat16)).astype(jnp.float32)

def reference(layer_input, grad_y, norm_gain, up_bias, up_tiles, down_tiles, block_cols, block_count):
    x_float = layer_input.astype(jnp.float32)
    norm_factor = lax.rsqrt(lax.optimization_barrier(jnp.mean(x_float * x_float, axis=-1, keepdims=True)) + NORM_EPS)
    x_unit = x_float * norm_factor
    normed = (x_unit * norm_gain[None, :]).astype(jnp.bfloat16)
    blocks_wide = D // BS
    group_size = FF // BS // N_COL
    group_rows = TOKENS // N_ROW
    slot_mask = (jnp.arange(KMAX, dtype=jnp.int32)[None, :] < block_count[:, None]).astype(jnp.float32)
    normed_blocks = normed.reshape(TOKENS, blocks_wide, BS)
    cotan_blocks = grad_y.reshape(TOKENS, blocks_wide, BS)
    pieces = (block_cols.reshape(N_COL, group_size, KMAX), slot_mask.reshape(N_COL, group_size, KMAX), up_tiles.reshape(N_COL, group_size, KMAX, BS, BS), down_tiles.reshape(N_COL, group_size, KMAX, BS, BS), up_bias.reshape(N_COL, group_size, BS))

    def one_group(running, piece):
        out_sum, in_sum = running
        columns, kept, w_up, w_down, bias_rows = piece
        kept_tiles = kept[:, :, None, None]
        up_float = w_up.astype(jnp.float32) * kept_tiles
        down_float = w_down.astype(jnp.float32) * kept_tiles
        picked_x = jnp.take(normed_blocks, columns, axis=1).astype(jnp.float32)
        picked_dy = jnp.take(cotan_blocks, columns, axis=1).astype(jnp.float32)
        hidden_pre = jnp.einsum('thkc,hkcd->thd', picked_x, up_float) + bias_rows[None]
        activated = rounded(gelu_tanh(hidden_pre))
        contrib = jnp.einsum('thc,hkcd->thkd', activated, down_float)
        out_part = jnp.zeros((TOKENS, blocks_wide, BS), jnp.float32).at[:, columns].add(contrib)
        act_grad = jnp.einsum('thkd,hkcd->thc', picked_dy, down_float)
        hidden_full = act_grad * gelu_slope(hidden_pre)
        bias_grad = lax.optimization_barrier(jnp.sum(hidden_full, axis=0))
        hidden_grad = rounded(hidden_full)
        act_rows = activated.reshape(N_ROW, group_rows, group_size, BS)
        dy_rows = picked_dy.reshape(N_ROW, group_rows, group_size, KMAX, BS)
        x_rows = picked_x.reshape(N_ROW, group_rows, group_size, KMAX, BS)
        grad_rows = hidden_grad.reshape(N_ROW, group_rows, group_size, BS)
        down_part = jnp.einsum('rthc,rthkd->rhkcd', act_rows, dy_rows) * kept_tiles[None]
        down_grad = lax.optimization_barrier(jnp.sum(rounded(down_part), axis=0))
        up_part = jnp.einsum('rthkc,rthd->rhkcd', x_rows, grad_rows) * kept_tiles[None]
        up_grad = lax.optimization_barrier(jnp.sum(rounded(up_part), axis=0))
        back = jnp.einsum('thd,hkcd->thkc', hidden_grad, up_float)
        in_part = jnp.zeros((TOKENS, blocks_wide, BS), jnp.float32).at[:, columns].add(back)
        running = (out_sum + rounded(out_part), in_sum + rounded(in_part))
        return (running, (up_grad, down_grad, bias_grad))
    start_sums = (jnp.zeros((TOKENS, blocks_wide, BS), jnp.float32), jnp.zeros((TOKENS, blocks_wide, BS), jnp.float32))
    (out_sum, in_sum), (up_grads, down_grads, bias_grads) = lax.scan(one_group, start_sums, pieces)
    layer_output = (x_float + out_sum.reshape(TOKENS, D)).astype(jnp.bfloat16)
    normed_grad = in_sum.reshape(TOKENS, D)
    grad_gain = lax.optimization_barrier(jnp.sum(normed_grad * x_unit, axis=0))
    scaled = normed_grad * norm_gain[None, :]
    inner = lax.optimization_barrier(jnp.mean(scaled * x_unit, axis=-1, keepdims=True))
    grad_x = (grad_y.astype(jnp.float32) + norm_factor * (scaled - x_unit * inner)).astype(jnp.bfloat16)
    grad_bias = bias_grads.reshape(FF)
    grad_up = up_grads.reshape(FF // BS, KMAX, BS, BS)
    grad_down = down_grads.reshape(FF // BS, KMAX, BS, BS)
    return (layer_output, grad_x, grad_gain, grad_bias, grad_up, grad_down)
```

```python
import math

import jax
import jax.numpy as jnp
from jax import lax
from jax.experimental import pallas as pl
from jax.experimental.pallas import tpu as pltpu
from jax.sharding import Mesh
from jax.sharding import PartitionSpec as P

D = 12288
HALF = D // 2
BS = 128
KMAX = 8
HID = 12
ROWS = 128
STRIP = 16

NORM_EPS = 1e-05
GELU_COEF = math.sqrt(2.0 / math.pi)
CUBIC_COEF = 0.044715
F32 = jnp.float32
BF16 = jnp.bfloat16


def shift(value, axis, steps):
    count = lax.axis_size(axis)
    return lax.ppermute(value, axis, [(i, (i + steps) % count) for i in range(count)])


def swap(value, axis, bit):
    count = lax.axis_size(axis)
    return lax.ppermute(value, axis, [(i, i ^ bit) for i in range(count)])


def dot(a, b, contract):
    return lax.dot_general(a, b, (contract, ((), ())), preferred_element_type=F32)


def compute_kernel(*refs):
    cols, core = refs[:2]
    tiles = refs[2:7]
    bias, gain = refs[7:9]
    near, far = refs[9:18], refs[18:27]
    keep, send = refs[27:35], refs[35:43]
    grads = refs[43:48]
    bias_sum, gain_sum = refs[48:50]
    x_all, dy_all, out_acc, in_acc, sems = refs[50:]

    mine = pl.multiple_of(core[0] * HALF, BS)
    other = pl.multiple_of((1 - core[0]) * HALF, BS)
    copies = []
    for pieces, start in ((near, mine), (far, other)):
        for which, target in ((0, x_all), (1, dy_all)):
            for j in range(8):
                source = pieces[j].at[which] if j < 7 else pieces[7 + which]
                copies.append(
                    pltpu.make_async_copy(
                        source,
                        target.at[pl.ds(j * STRIP, STRIP), pl.ds(start, HALF)],
                        sems.at[len(copies)],
                    )
                )
    for copy in copies:
        copy.start()
    out_acc[...] = jnp.zeros_like(out_acc)
    in_acc[...] = jnp.zeros_like(in_acc)
    for copy in copies:
        copy.wait()

    which = (0, 0, 1, 1, 2, 2, 3, 4)
    first = (0, 2 * HID, 0, 2 * HID, 0, 2 * HID, 0, 0)

    def hidden_block(i, carry):
        spans = [pl.ds(pl.multiple_of(cols[i, p] * BS, BS), BS) for p in range(KMAX)]
        x_pick = jnp.concatenate([x_all[:, s] for s in spans], axis=1)
        dy_pick = jnp.concatenate([dy_all[:, s] for s in spans], axis=1)
        up = jnp.concatenate([tiles[which[p]][first[p] + i] for p in range(KMAX)], axis=0)
        down = jnp.concatenate(
            [tiles[which[p]][first[p] + HID + i] for p in range(KMAX)], axis=1
        )
        hidden = dot(x_pick, up, ((1,), (0,))) + bias[i]
        act_grad = dot(dy_pick, down, ((1,), (1,)))
        squared = hidden * hidden
        bent = jnp.tanh(GELU_COEF * (hidden + CUBIC_COEF * squared * hidden))
        activated = (0.5 * hidden * (1.0 + bent)).astype(BF16)
        slope = 0.5 * (1.0 + bent) + 0.5 * hidden * (1.0 - bent * bent) * GELU_COEF * (
            1.0 + 3.0 * CUBIC_COEF * squared
        )
        hidden_full = act_grad * slope
        bias_sum[i] = jnp.sum(hidden_full, axis=0, keepdims=True)
        hidden_grad = hidden_full.astype(BF16)
        contrib = dot(activated, down, ((1,), (0,)))
        for p in range(KMAX):
            out_acc[:, spans[p]] += contrib[:, p * BS : (p + 1) * BS]
        down_grad = dot(activated, dy_pick, ((0,), (0,))).astype(BF16)
        back = dot(hidden_grad, up, ((1,), (1,)))
        for p in range(KMAX):
            in_acc[:, spans[p]] += back[:, p * BS : (p + 1) * BS]
        up_grad = dot(x_pick, hidden_grad, ((0,), (0,))).astype(BF16)
        for p in range(KMAX):
            grads[which[p]][first[p] + i] = up_grad[p * BS : (p + 1) * BS]
            grads[which[p]][first[p] + HID + i] = down_grad[:, p * BS : (p + 1) * BS]
        return carry

    lax.fori_loop(0, HID, hidden_block, 0)

    for j in range(8):
        rows = pl.ds(j * STRIP, STRIP)
        for part, acc in ((0, out_acc), (1, in_acc)):
            keep[j][part] = acc[rows, pl.ds(mine, HALF)].astype(BF16)
            send[j][part] = acc[rows, pl.ds(other, HALF)].astype(BF16)

    def gain_strip(b, carry):
        span = pl.ds(pl.multiple_of(b * 4 * BS, BS), 4 * BS)
        total = jnp.sum(in_acc[:, span] * x_all[:, span].astype(F32), axis=0, keepdims=True)
        gain_sum[:, span] = total / gain[:, span]
        return carry

    lax.fori_loop(0, D // (4 * BS), gain_strip, 0)


def compute(cols, core, tiles, bias, gain, near, far):
    vmem = pl.BlockSpec(memory_space=pltpu.VMEM)
    smem = pl.BlockSpec(memory_space=pltpu.SMEM)
    anyspace = pl.BlockSpec(memory_space=pl.ANY)
    part = jax.ShapeDtypeStruct((2, STRIP, HALF), BF16)
    out_shape = (
        [part] * 16
        + [jax.ShapeDtypeStruct(t.shape, BF16) for t in tiles]
        + [jax.ShapeDtypeStruct((HID, 1, BS), F32), jax.ShapeDtypeStruct((1, D), F32)]
    )
    outs = pl.pallas_call(
        compute_kernel,
        out_shape=out_shape,
        in_specs=[smem, smem] + [vmem] * 7 + [anyspace] * 18,
        out_specs=[vmem] * len(out_shape),
        scratch_shapes=[
            pltpu.VMEM((ROWS, D), BF16),
            pltpu.VMEM((ROWS, D), BF16),
            pltpu.VMEM((ROWS, D), F32),
            pltpu.VMEM((ROWS, D), F32),
            pltpu.SemaphoreType.DMA((32,)),
        ],
        compiler_params=pltpu.CompilerParams(vmem_limit_bytes=50 * 1024 * 1024),
        cost_estimate=pl.CostEstimate(
            flops=2_400_000_000, bytes_accessed=25_000_000, transcendentals=200_000
        ),
        name="butterfly_ffn",
    )(cols, core, *tiles, bias, gain, *near, *far)
    return outs[:8], outs[8:16], outs[16:21], outs[21], outs[22]


def add(a, b):
    return (a.astype(F32) + b.astype(F32)).astype(BF16)


def on_device(layer_input, grad_y, norm_gain, up_bias, up_tiles, down_tiles, block_cols, block_count):
    core = lax.axis_index("c")
    xi, yh = lax.axis_index("x"), lax.axis_index("yh")
    n_x = lax.axis_size("x")
    is_first = core == 0

    kept = (yh * n_x + xi < block_count).astype(BF16)[:, None, None]
    own_tiles = jnp.concatenate([up_tiles[:, 0] * kept, down_tiles[:, 0] * kept], axis=0)
    half_tiles = 2 * HID
    tiles_a = jnp.concatenate([own_tiles, swap(own_tiles, "yh", 1)], axis=0)
    tiles_r = shift(tiles_a, "x", 1)
    tiles_l = shift(tiles_a, "x", -1)
    tiles_h1 = shift(tiles_r[:half_tiles], "x", 1)
    tiles_h2 = shift(tiles_l[half_tiles:], "x", -1)
    left, right, across = (xi - 1) % n_x, (xi + 1) % n_x, (xi + 2) % n_x
    near_y, far_y = yh * n_x, (1 - yh) * n_x
    slots = jnp.stack(
        [near_y + xi, far_y + xi, near_y + left, far_y + left]
        + [near_y + right, far_y + right, near_y + across, far_y + across]
    )
    cols = jnp.take(block_cols, slots, axis=1)

    x_float = layer_input.astype(F32)
    norm_factor = lax.rsqrt(jnp.mean(x_float * x_float, axis=-1, keepdims=True) + NORM_EPS)
    x_unit = x_float * norm_factor
    normed = (x_unit * norm_gain[None, :]).astype(BF16)
    own = jnp.stack([normed, grad_y])
    low, high = own[:, :, :HALF], own[:, :, HALF:]
    mine = jnp.where(is_first, low, high)
    came = swap(jnp.where(is_first, high, low), "c", 1)
    pair = jnp.concatenate(
        [jnp.where(is_first, mine, came), jnp.where(is_first, came, mine)], axis=1
    )
    piece = jnp.concatenate([pair, swap(pair, "yl", 1)], axis=1)
    r1, l1 = shift(piece, "z", 1), shift(piece, "z", -1)
    r2, l2 = shift(r1, "z", 1), shift(l1, "z", -1)
    r3, l3 = shift(r2, "z", 1), shift(l2, "z", -1)
    x4, dy4 = shift(r3[0], "z", 1), shift(l3[1], "z", -1)
    near = [piece, r1, r2, r3, l1, l2, l3, x4, dy4]
    far = [swap(p, "c", 1) for p in near]

    keep, send, grads, bias_part, gain_part = compute(
        cols,
        core.reshape(1),
        [tiles_a, tiles_r, tiles_l, tiles_h1, tiles_h2],
        up_bias.reshape(HID, 1, BS),
        norm_gain[None, :],
        near,
        far,
    )

    g_a, g_r, g_l, g_h1, g_h2 = grads
    from_left, from_right = shift(g_h1, "x", 1), shift(g_h2, "x", -1)
    g_l = jnp.concatenate([add(g_l[:half_tiles], from_left), g_l[half_tiles:]], axis=0)
    g_r = jnp.concatenate([g_r[:half_tiles], add(g_r[half_tiles:], from_right)], axis=0)
    from_left, from_right = shift(g_l, "x", 1), shift(g_r, "x", -1)
    g_sum = g_a.astype(F32) + from_left.astype(F32) + from_right.astype(F32)
    came_g = swap(g_sum[half_tiles:].astype(BF16), "yh", 1)
    g_own = g_sum[:half_tiles] + came_g.astype(F32)
    kept_f = kept.astype(F32)
    grad_up = (g_own[:HID] * kept_f)[:, None]
    grad_down = (g_own[HID:] * kept_f)[:, None]

    sums = jnp.concatenate([gain_part[0], bias_part.reshape(HID * BS)])
    for axis, bit in (("yh", 1), ("x", 1), ("x", 2)):
        sums = sums + swap(sums, axis, bit)
    grad_bias = sums[D:]
    grad_gain = sums[:D]
    for axis, bit in (("c", 1), ("yl", 1), ("z", 1), ("z", 2), ("z", 4)):
        grad_gain = grad_gain + swap(grad_gain, axis, bit)

    parts = [add(k, swap(s, "c", 1)) for k, s in zip(keep, send, strict=True)]
    p0, m1, m2, m3, q1, q2, q3, p4 = parts
    up_half, down_half = shift(p4[0], "z", 1), shift(p4[1], "z", -1)
    q3 = jnp.stack([add(q3[0], up_half), q3[1]])
    m3 = jnp.stack([m3[0], add(m3[1], down_half)])
    up3, down3 = shift(q3, "z", 1), shift(m3, "z", -1)
    q2, m2 = add(q2, up3), add(m2, down3)
    up2, down2 = shift(q2, "z", 1), shift(m2, "z", -1)
    q1, m1 = add(q1, up2), add(m1, down2)
    up1, down1 = shift(q1, "z", 1), shift(m1, "z", -1)
    total = p0.astype(F32) + up1.astype(F32) + down1.astype(F32)
    eight = STRIP // 2
    came_y = swap(total[:, eight:].astype(BF16), "yl", 1)
    total = total[:, :eight] + came_y.astype(F32)
    four = eight // 2
    mine_t = jnp.where(is_first, total[:, :four], total[:, four:])
    send_t = jnp.where(is_first, total[:, four:], total[:, :four]).astype(BF16)
    came_t = swap(send_t, "c", 1).astype(F32)
    both = jnp.concatenate(
        [jnp.where(is_first, mine_t, came_t), jnp.where(is_first, came_t, mine_t)], axis=2
    )
    layer_output = (x_float + both[0]).astype(BF16)
    normed_grad = both[1]
    scaled = normed_grad * norm_gain[None, :]
    inner = jnp.mean(scaled * x_unit, axis=-1, keepdims=True)
    grad_x = (grad_y.astype(F32) + norm_factor * (scaled - x_unit * inner)).astype(BF16)
    return (layer_output, grad_x, grad_gain, grad_bias, grad_up, grad_down)


def solution(mesh):
    fine = Mesh(mesh.devices.reshape(2, 4, 2, 8, 2), ("yh", "x", "yl", "z", "c"))
    row, col = ("yh", "x"), ("yl", "z", "c")
    tokens = P(row + col, None)
    tiles = P(col, row, None, None)
    return jax.shard_map(
        on_device,
        mesh=fine,
        in_specs=(tokens, tokens, P(), P(col), tiles, tiles, P(col, None), P(col)),
        out_specs=(tokens, tokens, P(), P(col), tiles, tiles),
        check_vma=False,
    )
```

```python
import math

import jax
import jax.numpy as jnp
from jax import lax
from jax.experimental import pallas as pl
from jax.experimental.pallas import tpu as pltpu
from jax.sharding import Mesh
from jax.sharding import PartitionSpec as P

D = 12288
HALF = D // 2
BS = 128
KMAX = 8
HID = 12
ROWS = 128
STRIP = 16

NORM_EPS = 1e-05
GELU_COEF = math.sqrt(2.0 / math.pi)
CUBIC_COEF = 0.044715
F32 = jnp.float32
BF16 = jnp.bfloat16


def shift(value, axis, steps):
    count = lax.axis_size(axis)
    return lax.ppermute(value, axis, [(i, (i + steps) % count) for i in range(count)])


def swap(value, axis, bit):
    count = lax.axis_size(axis)
    return lax.ppermute(value, axis, [(i, i ^ bit) for i in range(count)])


def dot(a, b, contract):
    return lax.dot_general(a, b, (contract, ((), ())), preferred_element_type=F32)


def compute_kernel(*refs):
    cols, core = refs[:2]
    tiles = refs[2:12]
    bias, gain = refs[12:14]
    near, far = refs[14:23], refs[23:32]
    keep = refs[32:40]
    send_last, send_rest = refs[40:42]
    grads = refs[42:56]
    bias_sum, gain_sum = refs[56:58]
    x_all, dy_all, out_acc, in_acc, sems = refs[58:]

    mine = pl.multiple_of(core[0] * HALF, BS)
    other = pl.multiple_of((1 - core[0]) * HALF, BS)
    copies = []
    for pieces, start in ((near, mine), (far, other)):
        for which, target in ((0, x_all), (1, dy_all)):
            for j in range(8):
                source = pieces[j].at[which] if j < 7 else pieces[7 + which]
                copies.append(
                    pltpu.make_async_copy(
                        source,
                        target.at[pl.ds(j * STRIP, STRIP), pl.ds(start, HALF)],
                        sems.at[len(copies)],
                    )
                )
    for copy in copies:
        copy.start()
    out_acc[...] = jnp.zeros_like(out_acc)
    in_acc[...] = jnp.zeros_like(in_acc)
    for copy in copies:
        copy.wait()

    up_at = (0, 1, 2, 3, 4, 5, 6, 8)
    down_at = (0, 1, 2, 3, 4, 5, 7, 9)
    down_from = (HID,) * 6 + (0, 0)
    grad_up_at = (0, 1, 2, 4, 6, 8, 10, 12)
    grad_down_at = (0, 1, 3, 5, 7, 9, 11, 13)
    grad_down_from = (HID,) * 2 + (0,) * 6

    def hidden_block(i, carry):
        spans = [pl.ds(pl.multiple_of(cols[i, p] * BS, BS), BS) for p in range(KMAX)]
        x_pick = jnp.concatenate([x_all[:, s] for s in spans], axis=1)
        dy_pick = jnp.concatenate([dy_all[:, s] for s in spans], axis=1)
        up = jnp.concatenate([tiles[up_at[p]][i] for p in range(KMAX)], axis=0)
        down = jnp.concatenate(
            [tiles[down_at[p]][down_from[p] + i] for p in range(KMAX)], axis=1
        )
        hidden = dot(x_pick, up, ((1,), (0,))) + bias[i]
        act_grad = dot(dy_pick, down, ((1,), (1,)))
        squared = hidden * hidden
        bent = jnp.tanh(GELU_COEF * (hidden + CUBIC_COEF * squared * hidden))
        activated = (0.5 * hidden * (1.0 + bent)).astype(BF16)
        slope = 0.5 * (1.0 + bent) + 0.5 * hidden * (1.0 - bent * bent) * GELU_COEF * (
            1.0 + 3.0 * CUBIC_COEF * squared
        )
        hidden_full = act_grad * slope
        bias_sum[i] = jnp.sum(hidden_full, axis=0, keepdims=True)
        hidden_grad = hidden_full.astype(BF16)
        contrib = dot(activated, down, ((1,), (0,)))
        for p in range(KMAX):
            out_acc[:, spans[p]] += contrib[:, p * BS : (p + 1) * BS]
        down_grad = dot(activated, dy_pick, ((0,), (0,))).astype(BF16)
        back = dot(hidden_grad, up, ((1,), (1,)))
        for p in range(KMAX):
            in_acc[:, spans[p]] += back[:, p * BS : (p + 1) * BS]
        up_grad = dot(x_pick, hidden_grad, ((0,), (0,))).astype(BF16)
        for p in range(KMAX):
            grads[grad_up_at[p]][i] = up_grad[p * BS : (p + 1) * BS]
            grads[grad_down_at[p]][grad_down_from[p] + i] = down_grad[:, p * BS : (p + 1) * BS]
        return carry

    lax.fori_loop(0, HID, hidden_block, 0)

    for j in range(8):
        rows = pl.ds(j * STRIP, STRIP)
        for part, acc in ((0, out_acc), (1, in_acc)):
            keep[j][part] = acc[rows, pl.ds(mine, HALF)].astype(BF16)
            target = send_last.at[part] if j == 7 else send_rest.at[j, part]
            target[...] = acc[rows, pl.ds(other, HALF)].astype(BF16)

    def gain_strip(b, carry):
        span = pl.ds(pl.multiple_of(b * 4 * BS, BS), 4 * BS)
        total = jnp.sum(in_acc[:, span] * x_all[:, span].astype(F32), axis=0, keepdims=True)
        gain_sum[:, span] = total / gain[:, span]
        return carry

    lax.fori_loop(0, D // (4 * BS), gain_strip, 0)


def compute(cols, core, tiles, bias, gain, near, far):
    vmem = pl.BlockSpec(memory_space=pltpu.VMEM)
    smem = pl.BlockSpec(memory_space=pltpu.SMEM)
    anyspace = pl.BlockSpec(memory_space=pl.ANY)
    part = jax.ShapeDtypeStruct((2, STRIP, HALF), BF16)
    out_shape = (
        [part] * 9
        + [jax.ShapeDtypeStruct((7, 2, STRIP, HALF), BF16)]
        + [jax.ShapeDtypeStruct((2 * HID, BS, BS), BF16)] * 2
        + [jax.ShapeDtypeStruct((HID, BS, BS), BF16)] * 12
        + [jax.ShapeDtypeStruct((HID, 1, BS), F32), jax.ShapeDtypeStruct((1, D), F32)]
    )
    outs = pl.pallas_call(
        compute_kernel,
        out_shape=out_shape,
        in_specs=[smem, smem] + [vmem] * 12 + [anyspace] * 18,
        out_specs=[vmem] * len(out_shape),
        scratch_shapes=[
            pltpu.VMEM((ROWS, D), BF16),
            pltpu.VMEM((ROWS, D), BF16),
            pltpu.VMEM((ROWS, D), F32),
            pltpu.VMEM((ROWS, D), F32),
            pltpu.SemaphoreType.DMA((32,)),
        ],
        compiler_params=pltpu.CompilerParams(vmem_limit_bytes=50 * 1024 * 1024),
        cost_estimate=pl.CostEstimate(
            flops=2_400_000_000, bytes_accessed=25_000_000, transcendentals=200_000
        ),
        name="butterfly_ffn",
    )(cols, core, *tiles, bias, gain, *near, *far)
    return outs[:8], outs[8], outs[9], outs[10:24], outs[24], outs[25]


def add(a, b):
    return (a.astype(F32) + b.astype(F32)).astype(BF16)


def add3(*values):
    return sum(v.astype(F32) for v in values)


def together(*values):
    return lax.optimization_barrier(values)


def on_device(layer_input, grad_y, norm_gain, up_bias, up_tiles, down_tiles, block_cols, block_count):
    core = lax.axis_index("c")
    xi, yh = lax.axis_index("x"), lax.axis_index("yh")
    n_x = lax.axis_size("x")
    is_first = core == 0

    kept = (yh * n_x + xi < block_count).astype(BF16)[:, None, None]
    near_t = jnp.concatenate([up_tiles[:, 0] * kept, down_tiles[:, 0] * kept], axis=0)
    left, right, across = (xi - 1) % n_x, (xi + 1) % n_x, (xi + 2) % n_x
    near_y, far_y = yh * n_x, (1 - yh) * n_x
    slots = jnp.stack(
        [near_y + xi, far_y + xi, near_y + left, far_y + left]
        + [near_y + right, far_y + right, near_y + across, far_y + across]
    )
    cols = jnp.take(block_cols, slots, axis=1)

    x_float = layer_input.astype(F32)
    norm_factor = lax.rsqrt(jnp.mean(x_float * x_float, axis=-1, keepdims=True) + NORM_EPS)
    x_unit = x_float * norm_factor
    normed = (x_unit * norm_gain[None, :]).astype(BF16)
    own = jnp.stack([normed, grad_y])
    low, high = own[:, :, :HALF], own[:, :, HALF:]
    mine, theirs = jnp.where(is_first, low, high), jnp.where(is_first, high, low)

    near_r, near_l = shift(near_t, "x", 1), shift(near_t, "x", -1)
    far_t = swap(near_t, "yh", 1)
    came = swap(theirs, "c", 1)
    pair = jnp.concatenate(
        [jnp.where(is_first, mine, came), jnp.where(is_first, came, mine)], axis=1
    )
    piece = jnp.concatenate([pair, swap(pair, "yl", 1)], axis=1)
    r1, l1 = shift(piece, "z", 1), shift(piece, "z", -1)
    near_r, near_l, far_t, r1, l1 = together(near_r, near_l, far_t, r1, l1)
    far_r, far_l = shift(far_t, "x", 1), shift(far_t, "x", -1)
    near_h1, near_h2 = shift(near_r[:HID], "x", 1), shift(near_l[HID:], "x", -1)
    r2, l2 = shift(r1, "z", 1), shift(l1, "z", -1)
    r3, l3 = shift(r2, "z", 1), shift(l2, "z", -1)
    far_p = [swap(p, "c", 1) for p in (piece, r1, l1)]
    far_r, far_l, near_h1, near_h2, r3, l3, *far_p = together(
        far_r, far_l, near_h1, near_h2, r3, l3, *far_p
    )
    far_h1, far_h2 = shift(far_r[:HID], "x", 1), shift(far_l[HID:], "x", -1)
    x4, dy4 = shift(r3[0], "z", 1), shift(l3[1], "z", -1)
    c_r2, c_l2, c_r3, c_l3, c_x4, c_dy4 = [swap(p, "c", 1) for p in (r2, l2, r3, l3, x4, dy4)]
    near = [piece, r1, r2, r3, l1, l2, l3, x4, dy4]
    far = [far_p[0], far_p[1], c_r2, c_r3, far_p[2], c_l2, c_l3, c_x4, c_dy4]

    keep, send_last, send_rest, grads, bias_part, gain_part = compute(
        cols,
        core.reshape(1),
        [near_t, far_t, near_r, far_r, near_l, far_l, near_h1, near_h2, far_h1, far_h2],
        up_bias.reshape(HID, 1, BS),
        norm_gain[None, :],
        near,
        far,
    )
    g_n, g_f, nr_u, nr_d, fr_u, fr_d, nl_u, nl_d, fl_u, fl_d, nh_u, nh_d, fh_u, fh_d = grads
    grad_gain = gain_part[0]
    p0, m1, m2, m3, q1, q2, q3, p4 = keep

    from_fl, from_fr = shift(fh_u, "x", 1), shift(fh_d, "x", -1)
    from_nl, from_nr = shift(nh_u, "x", 1), shift(nh_d, "x", -1)
    last = swap(send_last, "c", 1)
    rest = swap(send_rest, "c", 1)
    grad_gain = grad_gain + swap(grad_gain, "c", 1)
    sums = jnp.concatenate([grad_gain, bias_part.reshape(HID * BS)])
    p4 = add(p4, last)
    p4, sums = together(p4, sums)
    up_half, down_half = shift(p4[0], "z", 1), shift(p4[1], "z", -1)
    came_s = swap(sums, "x", 1)
    up_half, down_half, came_s, from_fl, from_fr, from_nl, from_nr, rest = together(
        up_half, down_half, came_s, from_fl, from_fr, from_nl, from_nr, rest
    )
    sums = sums + came_s
    q3, m3 = add3(q3, rest[6]), add3(m3, rest[3])
    q3 = jnp.stack([q3[0] + up_half.astype(F32), q3[1]]).astype(BF16)
    m3 = jnp.stack([m3[0], m3[1] + down_half.astype(F32)]).astype(BF16)
    g_fl = jnp.concatenate([add(fl_u, from_fl), fl_d], axis=0)
    g_fr = jnp.concatenate([fr_u, add(fr_d, from_fr)], axis=0)
    from_fl, from_fr = shift(g_fl, "x", 1), shift(g_fr, "x", -1)
    up3, down3 = shift(q3, "z", 1), shift(m3, "z", -1)
    sums = sums + swap(sums, "x", 2)
    came_s = swap(sums, "yh", 1)
    from_fl, from_fr, up3, down3, came_s = together(from_fl, from_fr, up3, down3, came_s)
    sums = sums + came_s
    grad_bias, grad_gain = sums[D:], sums[:D]
    g_f = add3(g_f, from_fl, from_fr).astype(BF16)
    g_nl = jnp.concatenate([add(nl_u, from_nl), nl_d], axis=0)
    g_nr = jnp.concatenate([nr_u, add(nr_d, from_nr)], axis=0)
    from_nl, from_nr = shift(g_nl, "x", 1), shift(g_nr, "x", -1)
    from_y = swap(g_f, "yh", 1)
    q2, m2 = add3(q2, rest[5], up3).astype(BF16), add3(m2, rest[2], down3).astype(BF16)
    up2, down2 = shift(q2, "z", 1), shift(m2, "z", -1)
    came_s = swap(grad_gain, "yl", 1)
    up2, down2, came_s = together(up2, down2, came_s)
    grad_gain = grad_gain + came_s
    q1, m1 = add3(q1, rest[4], up2).astype(BF16), add3(m1, rest[1], down2).astype(BF16)
    up1, down1 = shift(q1, "z", 1), shift(m1, "z", -1)
    came_s = swap(grad_gain, "z", 1)
    up1, down1, came_s, from_nl, from_nr, from_y = together(
        up1, down1, came_s, from_nl, from_nr, from_y
    )
    grad_gain = grad_gain + came_s
    total = add3(p0, rest[0], up1, down1)
    eight = STRIP // 2
    came_y = swap(total[:, eight:].astype(BF16), "yl", 1)
    came_s = swap(grad_gain, "z", 2)
    came_y, came_s = together(came_y, came_s)
    grad_gain = grad_gain + came_s
    total = total[:, :eight] + came_y.astype(F32)
    four = eight // 2
    mine_t = jnp.where(is_first, total[:, :four], total[:, four:])
    send_t = jnp.where(is_first, total[:, four:], total[:, :four]).astype(BF16)
    came_t = swap(send_t, "c", 1).astype(F32)
    grad_gain = grad_gain + swap(grad_gain, "z", 4)
    both = jnp.concatenate(
        [jnp.where(is_first, mine_t, came_t), jnp.where(is_first, came_t, mine_t)], axis=2
    )
    layer_output = (x_float + both[0]).astype(BF16)
    normed_grad = both[1]
    scaled = normed_grad * norm_gain[None, :]
    inner = jnp.mean(scaled * x_unit, axis=-1, keepdims=True)
    grad_x = (grad_y.astype(F32) + norm_factor * (scaled - x_unit * inner)).astype(BF16)
    g_own = add3(g_n, from_nl, from_nr, from_y)
    kept_f = kept.astype(F32)
    grad_up = (g_own[:HID] * kept_f)[:, None]
    grad_down = (g_own[HID:] * kept_f)[:, None]
    return (layer_output, grad_x, grad_gain, grad_bias, grad_up, grad_down)


def solution(mesh):
    fine = Mesh(mesh.devices.reshape(2, 4, 2, 8, 2), ("yh", "x", "yl", "z", "c"))
    row, col = ("yh", "x"), ("yl", "z", "c")
    tokens = P(row + col, None)
    tiles = P(col, row, None, None)
    return jax.shard_map(
        on_device,
        mesh=fine,
        in_specs=(tokens, tokens, P(), P(col), tiles, tiles, P(col, None), P(col)),
        out_specs=(tokens, tokens, P(), P(col), tiles, tiles),
        check_vma=False,
    )
```

```python
import math

import jax
import jax.numpy as jnp
from jax import lax
from jax.experimental import pallas as pl
from jax.experimental.pallas import tpu as pltpu
from jax.sharding import Mesh
from jax.sharding import PartitionSpec as P

D = 12288
HALF = D // 2
BS = 128
KMAX = 8
HID = 12
ROWS = 128
STRIP = 16

NORM_EPS = 1e-05
GELU_COEF = math.sqrt(2.0 / math.pi)
CUBIC_COEF = 0.044715
F32 = jnp.float32
BF16 = jnp.bfloat16


def shift(value, axis, steps):
    count = lax.axis_size(axis)
    return lax.ppermute(value, axis, [(i, (i + steps) % count) for i in range(count)])


def swap(value, axis, bit):
    count = lax.axis_size(axis)
    return lax.ppermute(value, axis, [(i, i ^ bit) for i in range(count)])


def step_x(value, sign):
    n, cores = lax.axis_size("x"), lax.axis_size("c")
    pairs = [
        (i * cores + c, (i + (sign if c == 0 else -sign)) % n * cores + c)
        for i in range(n)
        for c in range(cores)
    ]
    return lax.ppermute(value, ("x", "c"), pairs)


def dot(a, b, contract):
    return lax.dot_general(a, b, (contract, ((), ())), preferred_element_type=F32)


def compute_kernel(*refs):
    cols, core = refs[:2]
    tiles = refs[2:8]
    bias, gain = refs[8:10]
    near, far = refs[10:19], refs[19:28]
    keep = refs[28:36]
    send_last, send_rest = refs[36:38]
    grads = refs[38:44]
    bias_sum, gain_sum = refs[44:46]
    x_all, dy_all, out_acc, in_acc, sems = refs[46:]

    mine = pl.multiple_of(core[0] * HALF, BS)
    other = pl.multiple_of((1 - core[0]) * HALF, BS)
    copies = []
    for pieces, start in ((near, mine), (far, other)):
        for which, target in ((0, x_all), (1, dy_all)):
            for j in range(8):
                source = pieces[j].at[which] if j < 7 else pieces[7 + which]
                copies.append(
                    pltpu.make_async_copy(
                        source,
                        target.at[pl.ds(j * STRIP, STRIP), pl.ds(start, HALF)],
                        sems.at[len(copies)],
                    )
                )
    for copy in copies:
        copy.start()
    out_acc[...] = jnp.zeros_like(out_acc)
    in_acc[...] = jnp.zeros_like(in_acc)
    for copy in copies:
        copy.wait()

    which = (0, 1, 2, 3, 4, 4, 5, 5)
    first = (0, 0, 0, 0, 0, 2 * HID, 0, 2 * HID)

    def hidden_block(i, carry):
        spans = [pl.ds(pl.multiple_of(cols[i, p] * BS, BS), BS) for p in range(KMAX)]
        x_pick = jnp.concatenate([x_all[:, s] for s in spans], axis=1)
        dy_pick = jnp.concatenate([dy_all[:, s] for s in spans], axis=1)
        up = jnp.concatenate([tiles[which[p]][first[p] + i] for p in range(KMAX)], axis=0)
        down = jnp.concatenate(
            [tiles[which[p]][first[p] + HID + i] for p in range(KMAX)], axis=1
        )
        hidden = dot(x_pick, up, ((1,), (0,))) + bias[i]
        act_grad = dot(dy_pick, down, ((1,), (1,)))
        squared = hidden * hidden
        bent = jnp.tanh(GELU_COEF * (hidden + CUBIC_COEF * squared * hidden))
        activated = (0.5 * hidden * (1.0 + bent)).astype(BF16)
        slope = 0.5 * (1.0 + bent) + 0.5 * hidden * (1.0 - bent * bent) * GELU_COEF * (
            1.0 + 3.0 * CUBIC_COEF * squared
        )
        hidden_full = act_grad * slope
        bias_sum[i] = jnp.sum(hidden_full, axis=0, keepdims=True)
        hidden_grad = hidden_full.astype(BF16)
        contrib = dot(activated, down, ((1,), (0,)))
        for p in range(KMAX):
            out_acc[:, spans[p]] += contrib[:, p * BS : (p + 1) * BS]
        down_grad = dot(activated, dy_pick, ((0,), (0,))).astype(BF16)
        back = dot(hidden_grad, up, ((1,), (1,)))
        for p in range(KMAX):
            in_acc[:, spans[p]] += back[:, p * BS : (p + 1) * BS]
        up_grad = dot(x_pick, hidden_grad, ((0,), (0,))).astype(BF16)
        for p in range(KMAX):
            grads[which[p]][first[p] + i] = up_grad[p * BS : (p + 1) * BS]
            grads[which[p]][first[p] + HID + i] = down_grad[:, p * BS : (p + 1) * BS]
        return carry

    lax.fori_loop(0, HID, hidden_block, 0)

    for j in range(8):
        rows = pl.ds(j * STRIP, STRIP)
        for part, acc in ((0, out_acc), (1, in_acc)):
            keep[j][part] = acc[rows, pl.ds(mine, HALF)].astype(BF16)
            target = send_last.at[part] if j == 7 else send_rest.at[j, part]
            target[...] = acc[rows, pl.ds(other, HALF)].astype(BF16)

    def gain_strip(b, carry):
        span = pl.ds(pl.multiple_of(b * 4 * BS, BS), 4 * BS)
        total = jnp.sum(in_acc[:, span] * x_all[:, span].astype(F32), axis=0, keepdims=True)
        gain_sum[:, span] = total / gain[:, span]
        return carry

    lax.fori_loop(0, D // (4 * BS), gain_strip, 0)


def compute(cols, core, tiles, bias, gain, near, far):
    vmem = pl.BlockSpec(memory_space=pltpu.VMEM)
    smem = pl.BlockSpec(memory_space=pltpu.SMEM)
    anyspace = pl.BlockSpec(memory_space=pl.ANY)
    part = jax.ShapeDtypeStruct((2, STRIP, HALF), BF16)
    out_shape = (
        [part] * 9
        + [jax.ShapeDtypeStruct((7, 2, STRIP, HALF), BF16)]
        + [jax.ShapeDtypeStruct(t.shape, BF16) for t in tiles]
        + [jax.ShapeDtypeStruct((HID, 1, BS), F32), jax.ShapeDtypeStruct((1, D), F32)]
    )
    outs = pl.pallas_call(
        compute_kernel,
        out_shape=out_shape,
        in_specs=[smem, smem] + [vmem] * 8 + [anyspace] * 18,
        out_specs=[vmem] * len(out_shape),
        scratch_shapes=[
            pltpu.VMEM((ROWS, D), BF16),
            pltpu.VMEM((ROWS, D), BF16),
            pltpu.VMEM((ROWS, D), F32),
            pltpu.VMEM((ROWS, D), F32),
            pltpu.SemaphoreType.DMA((32,)),
        ],
        compiler_params=pltpu.CompilerParams(vmem_limit_bytes=50 * 1024 * 1024),
        cost_estimate=pl.CostEstimate(
            flops=2_400_000_000, bytes_accessed=25_000_000, transcendentals=200_000
        ),
        name="butterfly_ffn",
    )(cols, core, *tiles, bias, gain, *near, *far)
    return outs[:8], outs[8], outs[9], outs[10:16], outs[16], outs[17]


def add(a, b):
    return (a.astype(F32) + b.astype(F32)).astype(BF16)


def add3(*values):
    return sum(v.astype(F32) for v in values)


def together(*values):
    return lax.optimization_barrier(values)


def on_device(layer_input, grad_y, norm_gain, up_bias, up_tiles, down_tiles, block_cols, block_count):
    core = lax.axis_index("c")
    xi, yh = lax.axis_index("x"), lax.axis_index("yh")
    n_x = lax.axis_size("x")
    is_first = core == 0

    kept = (yh * n_x + xi < block_count).astype(BF16)[:, None, None]
    near_t = jnp.concatenate([up_tiles[:, 0] * kept, down_tiles[:, 0] * kept], axis=0)
    across = (xi + 2) % n_x
    odd = jnp.where(is_first, xi - 1, xi + 1) % n_x
    odd_across = (odd + 2) % n_x
    near_y, far_y = yh * n_x, (1 - yh) * n_x
    slots = jnp.stack(
        [near_y + xi, far_y + xi, near_y + across, far_y + across]
        + [near_y + odd, near_y + odd_across, far_y + odd, far_y + odd_across]
    )
    cols = jnp.take(block_cols, slots, axis=1)

    x_float = layer_input.astype(F32)
    norm_factor = lax.rsqrt(jnp.mean(x_float * x_float, axis=-1, keepdims=True) + NORM_EPS)
    x_unit = x_float * norm_factor
    normed = (x_unit * norm_gain[None, :]).astype(BF16)
    own = jnp.stack([normed, grad_y])
    low, high = own[:, :, :HALF], own[:, :, HALF:]
    mine, theirs = jnp.where(is_first, low, high), jnp.where(is_first, high, low)

    near2_t = swap(near_t, "x", 2)
    far_t = swap(near_t, "yh", 1)
    came = swap(theirs, "c", 1)
    pair = jnp.concatenate(
        [jnp.where(is_first, mine, came), jnp.where(is_first, came, mine)], axis=1
    )
    piece = jnp.concatenate([pair, swap(pair, "yl", 1)], axis=1)
    r1, l1 = shift(piece, "z", 1), shift(piece, "z", -1)
    near2_t, far_t, r1, l1 = together(near2_t, far_t, r1, l1)
    near_odd = step_x(jnp.concatenate([near_t, near2_t], axis=0), 1)
    far2_t = swap(near2_t, "yh", 1)
    r2, l2 = shift(r1, "z", 1), shift(l1, "z", -1)
    c_piece, c_r1, c_l1 = [swap(p, "c", 1) for p in (piece, r1, l1)]
    r3, l3 = shift(r2, "z", 1), shift(l2, "z", -1)
    far2_t, near_odd, r3, l3, c_piece, c_r1, c_l1 = together(
        far2_t, near_odd, r3, l3, c_piece, c_r1, c_l1
    )
    far_odd = step_x(jnp.concatenate([far_t, far2_t], axis=0), 1)
    x4, dy4 = shift(r3[0], "z", 1), shift(l3[1], "z", -1)
    c_r2, c_l2, c_r3, c_l3, c_x4, c_dy4 = [swap(p, "c", 1) for p in (r2, l2, r3, l3, x4, dy4)]
    near = [piece, r1, r2, r3, l1, l2, l3, x4, dy4]
    far = [c_piece, c_r1, c_r2, c_r3, c_l1, c_l2, c_l3, c_x4, c_dy4]

    keep, send_last, send_rest, grads, bias_part, gain_part = compute(
        cols,
        core.reshape(1),
        [near_t, far_t, near2_t, far2_t, near_odd, far_odd],
        up_bias.reshape(HID, 1, BS),
        norm_gain[None, :],
        near,
        far,
    )
    g_n, g_f, g_n2, g_f2, g_no, g_fo = grads
    sums = jnp.concatenate([gain_part[0], bias_part.reshape(HID * BS)])
    p0, m1, m2, m3, q1, q2, q3, p4 = keep

    last = swap(send_last, "c", 1)
    rest = swap(send_rest, "c", 1)
    sums = sums + swap(sums, "x", 1)
    came_s = swap(sums, "x", 2)
    came_s, last, g_fo, g_no = together(came_s, last, g_fo, g_no)
    from_fo, from_no = step_x(g_fo, -1), step_x(g_no, -1)
    sums = sums + came_s
    p4 = add(p4, last)
    up_half, down_half = shift(p4[0], "z", 1), shift(p4[1], "z", -1)
    came_s = swap(sums, "yh", 1)
    up_half, down_half, came_s, rest = together(up_half, down_half, came_s, rest)
    sums = sums + came_s
    grad_bias, grad_gain = sums[D:], sums[:D]
    q3, m3 = add3(q3, rest[6]), add3(m3, rest[3])
    q3 = jnp.stack([q3[0] + up_half.astype(F32), q3[1]]).astype(BF16)
    m3 = jnp.stack([m3[0], m3[1] + down_half.astype(F32)]).astype(BF16)
    up3, down3 = shift(q3, "z", 1), shift(m3, "z", -1)
    came_s = swap(grad_gain, "yl", 1)
    up3, down3, came_s, from_fo = together(up3, down3, came_s, from_fo)
    g_f2 = add(g_f2, from_fo[2 * HID :])
    from_f2 = swap(g_f2, "yh", 1)
    grad_gain = grad_gain + came_s
    q2, m2 = add3(q2, rest[5], up3).astype(BF16), add3(m2, rest[2], down3).astype(BF16)
    up2, down2 = shift(q2, "z", 1), shift(m2, "z", -1)
    came_s = swap(grad_gain, "z", 1)
    g_f = add(g_f, from_fo[: 2 * HID])
    up2, down2, came_s, from_no, from_f2, g_f = together(
        up2, down2, came_s, from_no, from_f2, g_f
    )
    g_n2 = add3(g_n2, from_no[2 * HID :], from_f2).astype(BF16)
    from_n2 = swap(g_n2, "x", 2)
    from_f = swap(g_f, "yh", 1)
    grad_gain = grad_gain + came_s
    q1, m1 = add3(q1, rest[4], up2).astype(BF16), add3(m1, rest[1], down2).astype(BF16)
    up1, down1 = shift(q1, "z", 1), shift(m1, "z", -1)
    came_s = swap(grad_gain, "z", 2)
    up1, down1, came_s = together(up1, down1, came_s)
    grad_gain = grad_gain + came_s
    total = add3(p0, rest[0], up1, down1)
    eight = STRIP // 2
    came_y = swap(total[:, eight:].astype(BF16), "yl", 1)
    came_s = swap(grad_gain, "z", 4)
    came_y, came_s, from_n2, from_f = together(came_y, came_s, from_n2, from_f)
    grad_gain = grad_gain + came_s
    total = total[:, :eight] + came_y.astype(F32)
    four = eight // 2
    mine_t = jnp.where(is_first, total[:, :four], total[:, four:])
    send_t = jnp.where(is_first, total[:, four:], total[:, :four]).astype(BF16)
    came_t = swap(send_t, "c", 1).astype(F32)
    grad_gain = grad_gain + swap(grad_gain, "c", 1)
    both = jnp.concatenate(
        [jnp.where(is_first, mine_t, came_t), jnp.where(is_first, came_t, mine_t)], axis=2
    )
    layer_output = (x_float + both[0]).astype(BF16)
    normed_grad = both[1]
    scaled = normed_grad * norm_gain[None, :]
    inner = jnp.mean(scaled * x_unit, axis=-1, keepdims=True)
    grad_x = (grad_y.astype(F32) + norm_factor * (scaled - x_unit * inner)).astype(BF16)
    g_own = add3(g_n, from_no[: 2 * HID], from_n2, from_f)
    kept_f = kept.astype(F32)
    grad_up = (g_own[:HID] * kept_f)[:, None]
    grad_down = (g_own[HID:] * kept_f)[:, None]
    return (layer_output, grad_x, grad_gain, grad_bias, grad_up, grad_down)


def solution(mesh):
    fine = Mesh(mesh.devices.reshape(2, 4, 2, 8, 2), ("yh", "x", "yl", "z", "c"))
    row, col = ("yh", "x"), ("yl", "z", "c")
    tokens = P(row + col, None)
    tiles = P(col, row, None, None)
    return jax.shard_map(
        on_device,
        mesh=fine,
        in_specs=(tokens, tokens, P(), P(col), tiles, tiles, P(col, None), P(col)),
        out_specs=(tokens, tokens, P(), P(col), tiles, tiles),
        check_vma=False,
    )
```

```python
import math

import jax
import jax.numpy as jnp
from jax import lax
from jax.experimental import pallas as pl
from jax.experimental.pallas import tpu as pltpu
from jax.sharding import Mesh
from jax.sharding import PartitionSpec as P

D = 12288
HALF = D // 2
BS = 128
KMAX = 8
HID = 12
ROWS = 128
STRIP = 16

NORM_EPS = 1e-05
GELU_COEF = math.sqrt(2.0 / math.pi)
CUBIC_COEF = 0.044715
F32 = jnp.float32
BF16 = jnp.bfloat16


def shift(value, axis, steps):
    count = lax.axis_size(axis)
    return lax.ppermute(value, axis, [(i, (i + steps) % count) for i in range(count)])


def swap(value, axis, bit):
    count = lax.axis_size(axis)
    return lax.ppermute(value, axis, [(i, i ^ bit) for i in range(count)])


def step_x(value, sign):
    n, cores = lax.axis_size("x"), lax.axis_size("c")
    pairs = [
        (i * cores + c, (i + (sign if c == 0 else -sign)) % n * cores + c)
        for i in range(n)
        for c in range(cores)
    ]
    return lax.ppermute(value, ("x", "c"), pairs)


def dot(a, b, contract):
    return lax.dot_general(a, b, (contract, ((), ())), preferred_element_type=F32)


def compute_kernel(*refs):
    cols, core = refs[:2]
    tiles = refs[2:8]
    bias, gain = refs[8:10]
    near, far = refs[10:19], refs[19:28]
    keep = refs[28:36]
    send = refs[36]
    grads = refs[37:43]
    bias_sum, gain_sum = refs[43:45]
    x_all, dy_all, out_acc, in_acc, sems = refs[45:]

    mine = pl.multiple_of(core[0] * HALF, BS)
    other = pl.multiple_of((1 - core[0]) * HALF, BS)
    copies = []
    for pieces, start in ((near, mine), (far, other)):
        for which, target in ((0, x_all), (1, dy_all)):
            for j in range(8):
                source = pieces[j].at[which] if j < 7 else pieces[7 + which]
                copies.append(
                    pltpu.make_async_copy(
                        source,
                        target.at[pl.ds(j * STRIP, STRIP), pl.ds(start, HALF)],
                        sems.at[len(copies)],
                    )
                )
    for copy in copies:
        copy.start()
    out_acc[...] = jnp.zeros_like(out_acc)
    in_acc[...] = jnp.zeros_like(in_acc)
    for copy in copies:
        copy.wait()

    which = (0, 1, 2, 3, 4, 4, 5, 5)
    first = (0, 0, 0, 0, 0, 2 * HID, 0, 2 * HID)

    def hidden_block(i, carry):
        spans = [pl.ds(pl.multiple_of(cols[i, p] * BS, BS), BS) for p in range(KMAX)]
        x_pick = jnp.concatenate([x_all[:, s] for s in spans], axis=1)
        dy_pick = jnp.concatenate([dy_all[:, s] for s in spans], axis=1)
        up = jnp.concatenate([tiles[which[p]][first[p] + i] for p in range(KMAX)], axis=0)
        down = jnp.concatenate(
            [tiles[which[p]][first[p] + HID + i] for p in range(KMAX)], axis=1
        )
        hidden = dot(x_pick, up, ((1,), (0,))) + bias[i]
        act_grad = dot(dy_pick, down, ((1,), (1,)))
        squared = hidden * hidden
        bent = jnp.tanh(GELU_COEF * (hidden + CUBIC_COEF * squared * hidden))
        activated = (0.5 * hidden * (1.0 + bent)).astype(BF16)
        slope = 0.5 * (1.0 + bent) + 0.5 * hidden * (1.0 - bent * bent) * GELU_COEF * (
            1.0 + 3.0 * CUBIC_COEF * squared
        )
        hidden_full = act_grad * slope
        bias_sum[i] = jnp.sum(hidden_full, axis=0, keepdims=True)
        hidden_grad = hidden_full.astype(BF16)
        contrib = dot(activated, down, ((1,), (0,)))
        for p in range(KMAX):
            out_acc[:, spans[p]] += contrib[:, p * BS : (p + 1) * BS]
        down_grad = dot(activated, dy_pick, ((0,), (0,))).astype(BF16)
        back = dot(hidden_grad, up, ((1,), (1,)))
        for p in range(KMAX):
            in_acc[:, spans[p]] += back[:, p * BS : (p + 1) * BS]
        up_grad = dot(x_pick, hidden_grad, ((0,), (0,))).astype(BF16)
        for p in range(KMAX):
            grads[which[p]][first[p] + i] = up_grad[p * BS : (p + 1) * BS]
            grads[which[p]][first[p] + HID + i] = down_grad[:, p * BS : (p + 1) * BS]
        return carry

    lax.fori_loop(0, HID, hidden_block, 0)

    for j in range(8):
        rows = pl.ds(j * STRIP, STRIP)
        for part, acc in ((0, out_acc), (1, in_acc)):
            keep[j][part] = acc[rows, pl.ds(mine, HALF)].astype(BF16)
            send[j, part] = acc[rows, pl.ds(other, HALF)].astype(BF16)

    def gain_strip(b, carry):
        span = pl.ds(pl.multiple_of(b * 4 * BS, BS), 4 * BS)
        total = jnp.sum(in_acc[:, span] * x_all[:, span].astype(F32), axis=0, keepdims=True)
        gain_sum[:, span] = total / gain[:, span]
        return carry

    lax.fori_loop(0, D // (4 * BS), gain_strip, 0)


def compute(cols, core, tiles, bias, gain, near, far):
    vmem = pl.BlockSpec(memory_space=pltpu.VMEM)
    smem = pl.BlockSpec(memory_space=pltpu.SMEM)
    anyspace = pl.BlockSpec(memory_space=pl.ANY)
    part = jax.ShapeDtypeStruct((2, STRIP, HALF), BF16)
    out_shape = (
        [part] * 8
        + [jax.ShapeDtypeStruct((8, 2, STRIP, HALF), BF16)]
        + [jax.ShapeDtypeStruct(t.shape, BF16) for t in tiles]
        + [jax.ShapeDtypeStruct((HID, 1, BS), F32), jax.ShapeDtypeStruct((1, D), F32)]
    )
    outs = pl.pallas_call(
        compute_kernel,
        out_shape=out_shape,
        in_specs=[smem, smem] + [vmem] * 8 + [anyspace] * 18,
        out_specs=[vmem] * len(out_shape),
        scratch_shapes=[
            pltpu.VMEM((ROWS, D), BF16),
            pltpu.VMEM((ROWS, D), BF16),
            pltpu.VMEM((ROWS, D), F32),
            pltpu.VMEM((ROWS, D), F32),
            pltpu.SemaphoreType.DMA((32,)),
        ],
        compiler_params=pltpu.CompilerParams(vmem_limit_bytes=50 * 1024 * 1024),
        cost_estimate=pl.CostEstimate(
            flops=2_400_000_000, bytes_accessed=25_000_000, transcendentals=200_000
        ),
        name="butterfly_ffn",
    )(cols, core, *tiles, bias, gain, *near, *far)
    return outs[:8], outs[8], outs[9:15], outs[15], outs[16]


def add(a, b):
    return (a.astype(F32) + b.astype(F32)).astype(BF16)


def add3(*values):
    return sum(v.astype(F32) for v in values)


def together(*values):
    return lax.optimization_barrier(values)


def on_device(layer_input, grad_y, norm_gain, up_bias, up_tiles, down_tiles, block_cols, block_count):
    core = lax.axis_index("c")
    xi, yh = lax.axis_index("x"), lax.axis_index("yh")
    n_x = lax.axis_size("x")
    is_first = core == 0

    kept = (yh * n_x + xi < block_count).astype(BF16)[:, None, None]
    near_t = jnp.concatenate([up_tiles[:, 0] * kept, down_tiles[:, 0] * kept], axis=0)
    across = (xi + 2) % n_x
    odd = jnp.where(is_first, xi - 1, xi + 1) % n_x
    odd_across = (odd + 2) % n_x
    near_y, far_y = yh * n_x, (1 - yh) * n_x
    slots = jnp.stack(
        [near_y + xi, far_y + xi, near_y + across, far_y + across]
        + [near_y + odd, near_y + odd_across, far_y + odd, far_y + odd_across]
    )
    cols = jnp.take(block_cols, slots, axis=1)

    x_float = layer_input.astype(F32)
    norm_factor = lax.rsqrt(jnp.mean(x_float * x_float, axis=-1, keepdims=True) + NORM_EPS)
    x_unit = x_float * norm_factor
    normed = (x_unit * norm_gain[None, :]).astype(BF16)
    own = jnp.stack([normed, grad_y])
    low, high = own[:, :, :HALF], own[:, :, HALF:]
    mine, theirs = jnp.where(is_first, low, high), jnp.where(is_first, high, low)

    near2_t = swap(near_t, "x", 2)
    far_t = swap(near_t, "yh", 1)
    came = swap(theirs, "c", 1)
    pair = jnp.concatenate(
        [jnp.where(is_first, mine, came), jnp.where(is_first, came, mine)], axis=1
    )
    piece = jnp.concatenate([pair, swap(pair, "yl", 1)], axis=1)
    r1, l1 = shift(piece, "z", 1), shift(piece, "z", -1)
    near2_t, far_t, r1, l1 = together(near2_t, far_t, r1, l1)
    near_odd = step_x(jnp.concatenate([near_t, near2_t], axis=0), 1)
    far2_t = swap(near2_t, "yh", 1)
    r2, l2 = shift(r1, "z", 1), shift(l1, "z", -1)
    c_piece, c_r1, c_l1 = [swap(p, "c", 1) for p in (piece, r1, l1)]
    r3, l3 = shift(r2, "z", 1), shift(l2, "z", -1)
    far2_t, near_odd, r3, l3, c_piece, c_r1, c_l1 = together(
        far2_t, near_odd, r3, l3, c_piece, c_r1, c_l1
    )
    far_odd = step_x(jnp.concatenate([far_t, far2_t], axis=0), 1)
    x4, dy4 = shift(r3[0], "z", 1), shift(l3[1], "z", -1)
    c_r2, c_l2, c_r3, c_l3, c_x4, c_dy4 = [swap(p, "c", 1) for p in (r2, l2, r3, l3, x4, dy4)]
    near = [piece, r1, r2, r3, l1, l2, l3, x4, dy4]
    far = [c_piece, c_r1, c_r2, c_r3, c_l1, c_l2, c_l3, c_x4, c_dy4]

    keep, send, grads, bias_part, gain_part = compute(
        cols,
        core.reshape(1),
        [near_t, far_t, near2_t, far2_t, near_odd, far_odd],
        up_bias.reshape(HID, 1, BS),
        norm_gain[None, :],
        near,
        far,
    )
    g_n, g_f, g_n2, g_f2, g_no, g_fo = grads
    sums = jnp.concatenate([gain_part[0], bias_part.reshape(HID * BS)])
    p0, m1, m2, m3, q1, q2, q3, p4 = keep

    rest = swap(send, "c", 1)
    sums = sums + swap(sums, "x", 1)
    came_s = swap(sums, "x", 2)
    came_s, rest, g_fo, g_no = together(came_s, rest, g_fo, g_no)
    from_fo, from_no = step_x(g_fo, -1), step_x(g_no, -1)
    sums = sums + came_s
    p4 = add(p4, rest[7])
    up_half, down_half = shift(p4[0], "z", 1), shift(p4[1], "z", -1)
    came_s = swap(sums, "yh", 1)
    up_half, down_half, came_s = together(up_half, down_half, came_s)
    sums = sums + came_s
    grad_bias, grad_gain = sums[D:], sums[:D]
    q3, m3 = add3(q3, rest[6]), add3(m3, rest[3])
    q3 = jnp.stack([q3[0] + up_half.astype(F32), q3[1]]).astype(BF16)
    m3 = jnp.stack([m3[0], m3[1] + down_half.astype(F32)]).astype(BF16)
    up3, down3 = shift(q3, "z", 1), shift(m3, "z", -1)
    came_s = swap(grad_gain, "yl", 1)
    up3, down3, came_s, from_fo = together(up3, down3, came_s, from_fo)
    g_f2 = add(g_f2, from_fo[2 * HID :])
    from_f2 = swap(g_f2, "yh", 1)
    grad_gain = grad_gain + came_s
    q2, m2 = add3(q2, rest[5], up3).astype(BF16), add3(m2, rest[2], down3).astype(BF16)
    up2, down2 = shift(q2, "z", 1), shift(m2, "z", -1)
    came_s = swap(grad_gain, "z", 1)
    g_f = add(g_f, from_fo[: 2 * HID])
    up2, down2, came_s, from_no, from_f2, g_f = together(
        up2, down2, came_s, from_no, from_f2, g_f
    )
    g_n2 = add3(g_n2, from_no[2 * HID :], from_f2).astype(BF16)
    from_n2 = swap(g_n2, "x", 2)
    from_f = swap(g_f, "yh", 1)
    grad_gain = grad_gain + came_s
    q1, m1 = add3(q1, rest[4], up2).astype(BF16), add3(m1, rest[1], down2).astype(BF16)
    up1, down1 = shift(q1, "z", 1), shift(m1, "z", -1)
    came_s = swap(grad_gain, "z", 2)
    up1, down1, came_s = together(up1, down1, came_s)
    grad_gain = grad_gain + came_s
    total = add3(p0, rest[0], up1, down1)
    eight = STRIP // 2
    came_y = swap(total[:, eight:].astype(BF16), "yl", 1)
    came_s = swap(grad_gain, "z", 4)
    came_y, came_s, from_n2, from_f = together(came_y, came_s, from_n2, from_f)
    grad_gain = grad_gain + came_s
    total = total[:, :eight] + came_y.astype(F32)
    four = eight // 2
    mine_t = jnp.where(is_first, total[:, :four], total[:, four:])
    send_t = jnp.where(is_first, total[:, four:], total[:, :four]).astype(BF16)
    came_t = swap(send_t, "c", 1).astype(F32)
    grad_gain = grad_gain + swap(grad_gain, "c", 1)
    both = jnp.concatenate(
        [jnp.where(is_first, mine_t, came_t), jnp.where(is_first, came_t, mine_t)], axis=2
    )
    layer_output = (x_float + both[0]).astype(BF16)
    normed_grad = both[1]
    scaled = normed_grad * norm_gain[None, :]
    inner = jnp.mean(scaled * x_unit, axis=-1, keepdims=True)
    grad_x = (grad_y.astype(F32) + norm_factor * (scaled - x_unit * inner)).astype(BF16)
    g_own = add3(g_n, from_no[: 2 * HID], from_n2, from_f)
    kept_f = kept.astype(F32)
    grad_up = (g_own[:HID] * kept_f)[:, None]
    grad_down = (g_own[HID:] * kept_f)[:, None]
    return (layer_output, grad_x, grad_gain, grad_bias, grad_up, grad_down)


def solution(mesh):
    fine = Mesh(mesh.devices.reshape(2, 4, 2, 8, 2), ("yh", "x", "yl", "z", "c"))
    row, col = ("yh", "x"), ("yl", "z", "c")
    tokens = P(row + col, None)
    tiles = P(col, row, None, None)
    return jax.shard_map(
        on_device,
        mesh=fine,
        in_specs=(tokens, tokens, P(), P(col), tiles, tiles, P(col, None), P(col)),
        out_specs=(tokens, tokens, P(), P(col), tiles, tiles),
        check_vma=False,
    )
```
